32 devices in a mesh: ep: 8 (over z, x), tp: 4 (over y, core).
Axes of the slice: x: 2, y: 2, z: 4, core: 2. Of those that a mesh axis runs over, the one named last changes fastest.
Arguments:
- inputs: bfloat16 [2, 512, 2, 2048], P(None, 'ep'), may hold values from -6 to 6
- lengths: int32 [2, 2], replicated, may hold values from 128 to 512, as said below
- routes: int32 [2, 512, 2, 8], P(None, 'ep'), may hold values from 0 to 15, all different within a row; in each aligned block of 128 rows (0 to 127, 128 to 255, ..., all dimensions but the last counted through in order) at most 80 rows name the same one
- w_query: bfloat16 [2048, 2048], P('ep', 'tp'), may hold values from -0.125 to 0.125
- w_key: bfloat16 [2048, 2048], P('ep', 'tp'), may hold values from -0.125 to 0.125
- w_value: bfloat16 [2048, 2048], P('ep', 'tp'), may hold values from -0.125 to 0.125
- w_output: bfloat16 [2048, 2048], P('ep', 'tp'), may hold values from -3 to 3
- w_router: bfloat16 [2048, 16], P('ep'), may hold values from -0.0625 to 0.0625
- attn_gain: bfloat16 [2048], P('ep'), may hold values from 0.5 to 1.5
- moe_gain: bfloat16 [2048], P('ep'), may hold values from 0.5 to 1.5
- query_gain: bfloat16 [2048], P('ep'), may hold values from 0.5 to 1.5
- key_gain: bfloat16 [2048], P('ep'), may hold values from 0.5 to 1.5
- w_gate: bfloat16 [16, 2048, 1024], P('ep', None, 'tp'), may hold values from -0.125 to 0.125
- w_up: bfloat16 [16, 2048, 1024], P('ep', None, 'tp'), may hold values from -0.125 to 0.125
- w_down: bfloat16 [16, 1024, 2048], P('ep', 'tp'), may hold values from -4 to 4
- out_grad: bfloat16 [2, 512, 2, 2048], P(None, 'ep'), may hold values from -6 to 6
Outputs:
- out: bfloat16 [2, 512, 2, 2048], P(None, 'ep')
- input_grad: float32 [2, 512, 2, 2048], P(None, 'ep')
- grad_query: float32 [2048, 2048], P('ep', 'tp')
- grad_key: float32 [2048, 2048], P('ep', 'tp')
- grad_value: float32 [2048, 2048], P('ep', 'tp')
- grad_output: float32 [2048, 2048], P('ep', 'tp')
- grad_router: float32 [2048, 16], P('ep')
- grad_attn_gain: float32 [2048], P('ep')
- grad_moe_gain: float32 [2048], P('ep')
- grad_query_gain: float32 [2048], P('ep')
- grad_key_gain: float32 [2048], P('ep')
- grad_gate: float32 [16, 2048, 1024], P('ep', None, 'tp')
- grad_up: float32 [16, 2048, 1024], P('ep', None, 'tp')
- grad_down: float32 [16, 1024, 2048], P('ep', 'tp')
The draws below stay inside these ranges and needn't reach their ends.
Inputs may be any that keep to these rules, and one draw needn't show every extreme that they name: `lengths`: in each micro-batch one sequence, which one drawn from the seed, has all 512 slots valid. `routes`: A row names 8 different experts. In each aligned block of 128 rows (the rows of one device in one micro-batch, in the array's order) no expert is named by more than 80 rows, and in some block some expert by exactly 80.
All inputs are finite; a program needn't handle non-finite values.
Results may differ from the reference program's by a relative error of at most 0.024.
Values may be sent and summed in bfloat16 or wider, within the bound.
A program may use at most 320 MiB of HBM per device.

```python
import math
import jax
import jax.numpy as jnp
import numpy as np
from jax import lax

D = 2048
HEADS = 16
HEAD_DIM = 128
FF = 1024
TOPK = 8
SLOTS_DEV = 64
SEQ_MB = 2
MB = 2
EXPERTS = 16
SEQLEN = 512
MOST = 80
N_TP = 4


def draw_lengths(key, part):
    key = jax.random.fold_in(key, 11)
    length_key, pick_key = jax.random.split(key)
    drawn = jax.random.randint(length_key, (MB, SEQ_MB), SEQLEN // 4, SEQLEN + 1)
    longest = jax.random.randint(pick_key, (MB, 1), 0, SEQ_MB)
    marked = jnp.arange(SEQ_MB, dtype=jnp.int32)[None, :] == longest
    return jnp.where(marked, SEQLEN, drawn).astype(jnp.int32)


def block_scale(rng, extent, cuts, least, top_value):
    factor_of, own = 1.0, jax.random.fold_in(rng, 6)
    for dim, shards_of in cuts:
        heights = jnp.exp(jax.random.uniform(jax.random.fold_in(own, dim), (shards_of,), jnp.float32, least / len(cuts), top_value / len(cuts)))
        factor_of = factor_of * jnp.repeat(heights, extent[dim] // shards_of).reshape([-1 if axis == dim else 1 for axis in range(len(extent))])
    return factor_of


def assign_block(rng, own, number, rows, count, top, most, lean):
    ranking = jax.random.permutation(rng, count)
    heavy_load, common = load_shares(count, rows * top, most, lean, True), load_shares(count, rows * top, most, lean, False)
    places = jnp.arange(count)

    def named(tallies, turn):
        used = int((tallies > 0).sum())
        fixed = max(1, used // 4)
        moved = fixed + (places - fixed + turn * (used - fixed)) % max(1, count - fixed)
        return jnp.zeros((count,), jnp.int32).at[ranking[jnp.where(places < fixed, places, moved)]].set(jnp.asarray(tallies, jnp.int32))

    tallies = jnp.where(number % 4 == 0, named(heavy_load, number // 4), named(common, number - number // 4 - 1))
    mixed = jax.random.permutation(jax.random.fold_in(own, 3), count)
    donor, sink = mixed[0:count // 2 * 2:2], mixed[1:count // 2 * 2:2]
    slack = jnp.minimum(tallies[donor] - 1, most - tallies[sink]) // 2
    slack = jnp.where((donor == ranking[0]) | (sink == ranking[0]) | (tallies[sink] == 0), 0, jnp.maximum(slack, 0))
    moved = jax.random.randint(jax.random.fold_in(own, 4), (count // 2,), 0, 1 << 20) % (slack + 1)
    tallies = tallies.at[donor].add(-moved).at[sink].add(moved)
    members = jnp.searchsorted(jnp.cumsum(tallies), jnp.arange(rows * top), side="right").astype(jnp.int32)
    listing = members.reshape(top, rows).T
    listing = listing[jax.random.permutation(jax.random.fold_in(own, 1), rows)]
    turn = jax.random.randint(jax.random.fold_in(own, 2), (rows, 1), 0, top)
    return jnp.take_along_axis(listing, (jnp.arange(top)[None, :] + turn) % top, axis=1)


def load_shares(count, total, limit, slope, full):
    weights = [(1 << 20) // math.isqrt(standing ** slope) + 1 for standing in range(1, count + 1)]
    largest = limit if full else min(limit, max(-(-total // count), total * weights[0] // sum(weights)))
    least = 1 if total - largest >= count - 1 else 0
    counts, rest = [largest] + [least] * (count - 1), total - largest - least * (count - 1)
    while rest > 0:
        candidates = [i for i in range(1, count) if counts[i] < largest] or [i for i in range(1, count) if counts[i] < limit]
        whole, budget = sum([weights[i] for i in candidates]), rest
        for i in candidates:
            addition = min(limit - counts[i], max(1, budget * weights[i] // whole), rest)
            counts[i] = counts[i] + addition
            rest = rest - addition
    return np.array(counts)


def bell_draw(stream_key, dims, width, reach, cuts=(), held_as=jnp.bfloat16):
    values = jax.random.normal(stream_key, dims, jnp.float32) * width
    if len(cuts) > 0:
        values = block_scale(stream_key, dims, cuts, -0.22, 0.18) * values
    return jnp.clip(values, min=-reach, max=reach).astype(held_as)


def setup_inputs(seed: int = 0) -> dict:
    keys = jax.random.split(jax.random.key(seed), 17)
    inputs = bell_draw(keys[0], (MB, SEQLEN, SEQ_MB, D), 1.0, 6.0, ((1, 8),))
    lengths = draw_lengths(jax.random.fold_in(keys[16], 71), 0)
    routes_keys = jax.random.split(jax.random.fold_in(keys[2], 1), MB * SEQLEN * SEQ_MB // (SLOTS_DEV * SEQ_MB))
    routes_turns = jax.random.permutation(jax.random.fold_in(keys[2], 3), MB * SEQLEN * SEQ_MB // (SLOTS_DEV * SEQ_MB))
    routes = jax.vmap(lambda own, number: assign_block(jax.random.fold_in(keys[2], 2), own, number, SLOTS_DEV * SEQ_MB, EXPERTS, TOPK, MOST, 1))(routes_keys, routes_turns).reshape((MB, SEQLEN, SEQ_MB, TOPK))
    w_query = bell_draw(keys[3], (D, D), D ** -0.5, 0.125, ((0, 8), (1, 4)))
    w_key = bell_draw(keys[4], (D, D), D ** -0.5, 0.125, ((0, 8), (1, 4)))
    w_value = bell_draw(keys[5], (D, D), D ** -0.5, 0.125, ((0, 8), (1, 4)))
    w_output = bell_draw(keys[6], (D, D), 0.5, 3.0, ((0, 8), (1, 4)))
    w_router = bell_draw(keys[7], (D, EXPERTS), (4 * D) ** -0.5, 0.0625, ((0, 8),))
    attn_gain = jnp.clip(1.0 + 0.1 * jax.random.normal(keys[8], (D,), jnp.float32), 0.5, 1.5).astype(jnp.bfloat16)
    moe_gain = jnp.clip(1.0 + 0.1 * jax.random.normal(keys[9], (D,), jnp.float32), 0.5, 1.5).astype(jnp.bfloat16)
    query_gain = jnp.clip(1.0 + 0.1 * jax.random.normal(keys[10], (D,), jnp.float32), 0.5, 1.5).astype(jnp.bfloat16)
    key_gain = jnp.clip(1.0 + 0.1 * jax.random.normal(keys[11], (D,), jnp.float32), 0.5, 1.5).astype(jnp.bfloat16)
    w_gate = bell_draw(keys[12], (EXPERTS, D, FF), D ** -0.5, 0.125, ((0, 8), (2, 4)))
    w_up = bell_draw(keys[13], (EXPERTS, D, FF), D ** -0.5, 0.125, ((0, 8), (2, 4)))
    w_down = bell_draw(keys[14], (EXPERTS, FF, D), 0.75, 4.0, ((0, 8), (1, 4)))
    out_grad = bell_draw(keys[15], (MB, SEQLEN, SEQ_MB, D), 1.0, 6.0, ((1, 8),))
    return dict(inputs=inputs, lengths=lengths, routes=routes, w_query=w_query, w_key=w_key, w_value=w_value, w_output=w_output, w_router=w_router, attn_gain=attn_gain, moe_gain=moe_gain, query_gain=query_gain, key_gain=key_gain, w_gate=w_gate, w_up=w_up, w_down=w_down, out_grad=out_grad)


@jax.custom_vjp
def low(v):
    return lax.optimization_barrier(v.astype(jnp.bfloat16)).astype(jnp.float32)

@jax.custom_vjp
def low_back(v):
    return v

def low_keep(v):
    return (low(v), None)

def low_pass(kept, grad):
    return (grad,)

def back_keep(v):
    return (v, None)

def back_low(kept, grad):
    return (low(grad),)
low.defvjp(low_keep, low_pass)
low_back.defvjp(back_keep, back_low)
EPSILON = 1e-05
THETA_BASE = 10000.0
NEGATIVE = -1e+30

def matmul(left, right):
    return jnp.dot(left, right, preferred_element_type=jnp.float32, precision=lax.Precision.HIGHEST)

def row_scale(values):
    return lax.rsqrt(lax.optimization_barrier(jnp.mean(values * values, axis=-1, keepdims=True)) + EPSILON)

def turn_half(values):
    half_width = values.shape[-1] // 2
    return jnp.concatenate([-values[..., half_width:], values[..., :half_width]], axis=-1)

def rope_tables(first_place, place_count):
    half_width = HEAD_DIM // 2
    places = (first_place + jnp.arange(place_count, dtype=jnp.int32)).astype(jnp.float32)
    inverse = THETA_BASE ** (-jnp.arange(half_width, dtype=jnp.float32) * 2.0 / HEAD_DIM)
    angles = places[:, None] * inverse[None, :]
    angles = jnp.concatenate([angles, angles], axis=-1)
    return (jnp.cos(angles), jnp.sin(angles))

def rotate_forth(values, cosine_table, sine_table):
    return values * cosine_table + turn_half(values) * sine_table

def attend_sequence(sequence_item):
    queries, key_rows, value_rows, length = sequence_item
    positions = jnp.arange(SEQLEN, dtype=jnp.int32)
    allowed = (positions[None, :] <= positions[:, None]) & (positions[None, :] < length)
    score_scale = HEAD_DIM ** (-0.5)

    def one_head(head_item):
        query_head, key_head, value_head = head_item
        scores = low_back(matmul(query_head, key_head.T) * score_scale)
        scores = jnp.where(allowed, scores, NEGATIVE)
        return matmul(low(jax.nn.softmax(scores, axis=-1)), value_head)
    return lax.map(jax.checkpoint(one_head), (queries, key_rows, value_rows))

def reference(inputs, lengths, routes, w_query, w_key, w_value, w_output, w_router, attn_gain, moe_gain, query_gain, key_gain, w_gate, w_up, w_down, out_grad):
    expert_numbers = jnp.arange(EXPERTS, dtype=jnp.int32)
    chosen = jnp.any(routes[..., None] == expert_numbers, axis=-2).reshape(-1, EXPERTS).astype(jnp.float32)
    positions = jnp.arange(SEQLEN, dtype=jnp.int32)
    valid = (positions[None, :, None] < lengths[:, None, :]).astype(jnp.float32).reshape(-1)
    cosine_table, sine_table = rope_tables(0, SEQLEN)
    cosine_table = cosine_table[None, :, None, None, :]
    sine_table = sine_table[None, :, None, None, :]
    row_total = MB * SEQLEN * SEQ_MB
    head_shape = (MB, SEQLEN, SEQ_MB, HEADS, HEAD_DIM)
    block_width = FF // N_TP

    def by_sequence(values):
        ordered = jnp.transpose(values.reshape(head_shape), (0, 2, 3, 1, 4))
        return ordered.reshape(MB * SEQ_MB, HEADS, SEQLEN, HEAD_DIM)

    def layer(hidden_in, query_weight, key_weight, value_weight, output_weight, router_weight, gain_attn, gain_moe, gain_query, gain_key, gate_weight, up_weight, down_weight):
        flat_in = hidden_in.reshape(row_total, D)
        normed_in = low(flat_in * row_scale(flat_in) * gain_attn)
        query_pre = low_back(matmul(normed_in, query_weight))
        key_pre = low_back(matmul(normed_in, key_weight))
        value_rows = low_back(low(matmul(normed_in, value_weight)))
        query_normed = query_pre * row_scale(query_pre) * gain_query
        key_normed = key_pre * row_scale(key_pre) * gain_key
        query_turned = low(rotate_forth(query_normed.reshape(head_shape), cosine_table, sine_table))
        key_turned = low(rotate_forth(key_normed.reshape(head_shape), cosine_table, sine_table))
        attended = lax.map(jax.checkpoint(attend_sequence), (by_sequence(query_turned), by_sequence(key_turned), by_sequence(value_rows), lengths.reshape(-1)))
        attended = attended.reshape(MB, SEQ_MB, HEADS, SEQLEN, HEAD_DIM)
        attended = jnp.transpose(attended, (0, 3, 1, 2, 4)).reshape(row_total, D)
        attended = low_back(low(attended))
        attn_rows = low_back(matmul(attended, output_weight.T))
        middle = flat_in + attn_rows
        normed_mid = low(middle * row_scale(middle) * gain_moe)
        logits = low_back(matmul(normed_mid, router_weight))
        shares = jax.nn.softmax(logits, axis=-1) * chosen

        def expert_step(running, expert_item):
            gate_part, up_part, down_part, expert_share = expert_item
            gate_in = low_back(matmul(normed_mid, gate_part))
            up_in = low_back(matmul(normed_mid, up_part))
            active = low(jax.nn.silu(gate_in) * up_in)
            summed = jnp.zeros((row_total, D), jnp.float32)
            for quarter in range(N_TP):
                lower_edge = quarter * block_width
                upper_edge = (quarter + 1) * block_width
                summed = summed + low(matmul(active[:, lower_edge:upper_edge], down_part[lower_edge:upper_edge]))
            return (running + expert_share[:, None] * low_back(summed), None)
        mixed = lax.scan(jax.checkpoint(expert_step), jnp.zeros((row_total, D), jnp.float32), (gate_weight, up_weight, down_weight, shares.T))[0]
        return ((middle + mixed) * valid[:, None]).reshape(hidden_in.shape)
    result, pull_back = jax.vjp(layer, inputs.astype(jnp.float32), w_query.astype(jnp.float32), w_key.astype(jnp.float32), w_value.astype(jnp.float32), w_output.astype(jnp.float32), w_router.astype(jnp.float32), attn_gain.astype(jnp.float32), moe_gain.astype(jnp.float32), query_gain.astype(jnp.float32), key_gain.astype(jnp.float32), w_gate.astype(jnp.float32), w_up.astype(jnp.float32), w_down.astype(jnp.float32))
    grads = pull_back(out_grad.astype(jnp.float32))
    return (result.astype(jnp.bfloat16), grads[0], grads[1], grads[2], grads[3], grads[4], grads[5], grads[6], grads[7], grads[8], grads[9], grads[10], grads[11], grads[12])
```

```python
import jax
import jax.numpy as jnp
import numpy as np
from jax import lax
from jax.experimental import pallas as pl
from jax.experimental.pallas import tpu as pltpu
from jax.sharding import PartitionSpec as P

HEAD_DIM = 128


EPSILON = 1e-05
THETA_BASE = 10000.0
NEGATIVE = -1e30


def row_scale(values):
    return lax.rsqrt(jnp.mean(values * values, axis=-1, keepdims=True) + EPSILON)


def turn_half(values):
    half_width = values.shape[-1] // 2
    return jnp.concatenate([-values[..., half_width:], values[..., :half_width]], axis=-1)


def rope_tables(first_place, place_count):
    half_width = HEAD_DIM // 2
    places = (first_place + jnp.arange(place_count, dtype=jnp.int32)).astype(jnp.float32)
    inverse = THETA_BASE ** (-jnp.arange(half_width, dtype=jnp.float32) * 2.0 / HEAD_DIM)
    angles = places[:, None] * inverse[None, :]
    angles = jnp.concatenate([angles, angles], axis=-1)
    return (jnp.cos(angles), jnp.sin(angles))


def rotate_forth(values, cosine_table, sine_table):
    return values * cosine_table + turn_half(values) * sine_table


def rotate_back(values, cosine_table, sine_table):
    return values * cosine_table - turn_half(values) * sine_table


def allowed_table(first_place, query_count, key_count, length):
    query_place = first_place + jnp.arange(query_count, dtype=jnp.int32)
    key_place = jnp.arange(key_count, dtype=jnp.int32)
    return (key_place[None, :] <= query_place[:, None]) & (key_place[None, :] < length)


def attend_forward(queries, key_rows, value_rows, first_place, length, score_scale):
    allowed = allowed_table(first_place, queries.shape[0], key_rows.shape[0], length)
    scores = (
        jnp.einsum("chd,lhd->hcl", queries, key_rows, preferred_element_type=jnp.float32)
        * score_scale
    )
    scores = jnp.where(allowed[None], scores, NEGATIVE)
    highest = jnp.max(scores, axis=-1, keepdims=True)
    weights = jnp.exp(scores - highest)
    totals = jnp.sum(weights, axis=-1, keepdims=True)
    probability = (weights / totals).astype(jnp.bfloat16)
    attended = jnp.einsum(
        "hcl,lhd->chd", probability, value_rows, preferred_element_type=jnp.float32
    )
    return (attended, (highest + jnp.log(totals))[..., 0])


def attend_backward(
    queries, key_rows, value_rows, attended_grad, log_total, first_place, length, score_scale
):
    allowed = allowed_table(first_place, queries.shape[0], key_rows.shape[0], length)
    scores = (
        jnp.einsum("chd,lhd->hcl", queries, key_rows, preferred_element_type=jnp.float32)
        * score_scale
    )
    scores = jnp.where(allowed[None], scores, NEGATIVE)
    probability = jnp.exp(scores - log_total[..., None])
    prob_grad = jnp.einsum(
        "chd,lhd->hcl", attended_grad, value_rows, preferred_element_type=jnp.float32
    )
    centre = jnp.sum(probability * prob_grad, axis=-1, keepdims=True)
    score_grad = (probability * (prob_grad - centre)).astype(jnp.bfloat16)
    query_grad = (
        jnp.einsum("hcl,lhd->chd", score_grad, key_rows, preferred_element_type=jnp.float32)
        * score_scale
    )
    key_grad = (
        jnp.einsum("hcl,chd->lhd", score_grad, queries, preferred_element_type=jnp.float32)
        * score_scale
    )
    value_grad = jnp.einsum(
        "hcl,chd->lhd",
        probability.astype(jnp.bfloat16),
        attended_grad,
        preferred_element_type=jnp.float32,
    )
    return (query_grad, key_grad, value_grad, centre[..., 0])


def gather_keys(key_blocks, value_blocks):
    return (
        lax.all_gather(key_blocks, "ep", axis=0, tiled=True),
        lax.all_gather(value_blocks, "ep", axis=0, tiled=True),
    )


def contract_rows(left, right):
    return lax.dot_general(
        left, right, (((0,), (0,)), ((), ())), preferred_element_type=jnp.float32
    )


def contract_cols(left, right):
    return lax.dot_general(
        left, right, (((1,), (1,)), ((), ())), preferred_element_type=jnp.float32
    )


def routed_shards(
    inputs,
    lengths,
    routes,
    w_query,
    w_key,
    w_value,
    w_output,
    w_router,
    attn_gain,
    moe_gain,
    query_gain,
    key_gain,
    w_gate,
    w_up,
    w_down,
    out_grad,
):
    micro_count, block_rows, sequence_count, width = inputs.shape
    axis_devices = lax.axis_size("ep")
    shard_index = lax.axis_index("ep")
    hidden_index = lax.axis_index("tp")
    local_width = w_query.shape[1]
    local_heads = local_width // HEAD_DIM
    local_experts = w_gate.shape[0]
    expert_count = local_experts * axis_devices
    top_count = routes.shape[-1]
    row_count = block_rows * sequence_count
    sequence_length = block_rows * axis_devices
    capacity = 5 * row_count * top_count // (4 * expert_count)
    score_scale = HEAD_DIM ** (-0.5)
    first_place = shard_index * block_rows
    cosine_table, sine_table = rope_tables(first_place, block_rows)
    cosine_table = cosine_table[:, None, None, :]
    sine_table = sine_table[:, None, None, :]
    local_place = first_place + jnp.arange(block_rows, dtype=jnp.int32)
    expert_numbers = jnp.arange(expert_count, dtype=jnp.int32)
    zero_width = jnp.zeros((width,), jnp.float32)
    head_shape = (block_rows, sequence_count, local_heads, HEAD_DIM)
    grad_query = jnp.zeros((width, local_width), jnp.float32)
    grad_key = jnp.zeros((width, local_width), jnp.float32)
    grad_value = jnp.zeros((width, local_width), jnp.float32)
    grad_output = jnp.zeros((width, local_width), jnp.float32)
    grad_router = jnp.zeros((width, expert_count), jnp.float32)
    grad_gain_attn = zero_width
    grad_gain_moe = zero_width
    grad_gain_query = zero_width
    grad_gain_key = zero_width
    grad_gate = jnp.zeros(w_gate.shape, jnp.float32)
    grad_up = jnp.zeros(w_up.shape, jnp.float32)
    grad_down = jnp.zeros(w_down.shape, jnp.float32)
    outputs_list = []
    input_grads = []
    for micro_index in range(micro_count):
        gathered = (
            lax.all_gather(w_query, "ep", axis=0, tiled=True),
            lax.all_gather(w_key, "ep", axis=0, tiled=True),
            lax.all_gather(w_value, "ep", axis=0, tiled=True),
            lax.all_gather(w_output, "ep", axis=0, tiled=True),
            lax.all_gather(w_router, "ep", axis=0, tiled=True),
            lax.all_gather(attn_gain, "ep", axis=0, tiled=True),
            lax.all_gather(moe_gain, "ep", axis=0, tiled=True),
            lax.all_gather(query_gain, "ep", axis=0, tiled=True),
            lax.all_gather(key_gain, "ep", axis=0, tiled=True),
        )
        full_query, full_key, full_value, full_output, full_router = (
            gathered[0],
            gathered[1],
            gathered[2],
            gathered[3],
            gathered[4],
        )
        gain_attn = gathered[5].astype(jnp.float32)
        gain_moe = gathered[6].astype(jnp.float32)
        gain_query = lax.dynamic_slice_in_dim(
            gathered[7].astype(jnp.float32), hidden_index * local_width, local_width
        )
        gain_key = lax.dynamic_slice_in_dim(
            gathered[8].astype(jnp.float32), hidden_index * local_width, local_width
        )
        hidden_in = inputs[micro_index].reshape(row_count, width).astype(jnp.float32)
        scale_in = row_scale(hidden_in)
        normed_in = (hidden_in * scale_in * gain_attn).astype(jnp.bfloat16)
        query_pre = jnp.dot(normed_in, full_query, preferred_element_type=jnp.float32)
        key_pre = jnp.dot(normed_in, full_key, preferred_element_type=jnp.float32)
        value_rows = jnp.dot(normed_in, full_value, preferred_element_type=jnp.float32).astype(
            jnp.bfloat16
        )
        query_square, key_square = lax.psum(
            (jnp.sum(query_pre * query_pre, axis=1), jnp.sum(key_pre * key_pre, axis=1)), "tp"
        )
        query_scale = lax.rsqrt(query_square / width + EPSILON)[:, None]
        key_scale = lax.rsqrt(key_square / width + EPSILON)[:, None]
        query_turned = rotate_forth(
            (query_pre * query_scale * gain_query).reshape(head_shape), cosine_table, sine_table
        ).astype(jnp.bfloat16)
        key_turned = rotate_forth(
            (key_pre * key_scale * gain_key).reshape(head_shape), cosine_table, sine_table
        ).astype(jnp.bfloat16)
        key_blocks = key_turned.reshape(block_rows, sequence_count, local_width)
        value_blocks = value_rows.reshape(block_rows, sequence_count, local_width)
        key_all, value_all = gather_keys(key_blocks, value_blocks)
        attended_list = []
        log_totals = []
        for sequence in range(sequence_count):
            attended_one, log_one = attend_forward(
                query_turned[:, sequence],
                key_all[:, sequence].reshape(sequence_length, local_heads, HEAD_DIM),
                value_all[:, sequence].reshape(sequence_length, local_heads, HEAD_DIM),
                first_place,
                lengths[micro_index, sequence],
                score_scale,
            )
            attended_list.append(attended_one)
            log_totals.append(log_one)
        attended = (
            jnp.stack(attended_list, axis=1).reshape(row_count, local_width).astype(jnp.bfloat16)
        )
        attn_rows = lax.psum(contract_cols(attended, full_output), "tp")
        middle = hidden_in + attn_rows
        scale_mid = row_scale(middle)
        normed_mid = (middle * scale_mid * gain_moe).astype(jnp.bfloat16)
        logits = jnp.dot(normed_mid, full_router, preferred_element_type=jnp.float32)
        probs = jax.nn.softmax(logits, axis=-1)
        named_rows = routes[micro_index].reshape(row_count, top_count)
        picked = named_rows[:, :, None] == expert_numbers[None, None, :]
        picked_float = picked.astype(jnp.float32)
        gates = jnp.sum(picked_float * probs[:, None, :], axis=-1)
        chosen_rows = jnp.sum(picked_float, axis=1)
        before = jnp.arange(row_count)[:, None] > jnp.arange(row_count)[None, :]
        earlier = jnp.dot(
            before.astype(jnp.bfloat16),
            chosen_rows.astype(jnp.bfloat16),
            preferred_element_type=jnp.float32,
        )
        places = jnp.sum(picked_float * earlier[:, None, :], axis=-1).astype(jnp.int32).reshape(-1)
        slots = named_rows.reshape(-1) * capacity + places
        outgoing = (
            jnp.zeros((expert_count * capacity, width), jnp.bfloat16)
            .at[slots]
            .set(jnp.repeat(normed_mid, top_count, axis=0))
        )
        arrived = lax.all_to_all(
            outgoing.reshape(axis_devices, local_experts, capacity, width),
            "ep",
            split_axis=0,
            concat_axis=0,
            tiled=True,
        )
        gate_in = jnp.einsum("secd,edf->secf", arrived, w_gate, preferred_element_type=jnp.float32)
        up_in = jnp.einsum("secd,edf->secf", arrived, w_up, preferred_element_type=jnp.float32)
        active = jax.nn.silu(gate_in)
        inner = (active * up_in).astype(jnp.bfloat16)
        partial_out = jnp.einsum(
            "secf,efd->secd", inner, w_down, preferred_element_type=jnp.float32
        ).astype(jnp.bfloat16)
        returned = lax.all_to_all(
            partial_out, "ep", split_axis=0, concat_axis=0, tiled=True
        ).reshape(expert_count * capacity, width)
        picked_rows = returned[slots].reshape(row_count, top_count, width)
        moe_part = jnp.sum(gates[:, :, None] * picked_rows.astype(jnp.float32), axis=1)
        moe_rows = lax.psum(moe_part.astype(jnp.bfloat16), "tp").astype(jnp.float32)
        valid = (
            (local_place[:, None] < lengths[micro_index][None, :])
            .astype(jnp.float32)
            .reshape(row_count)
        )
        outputs_list.append(
            ((middle + moe_rows) * valid[:, None])
            .astype(jnp.bfloat16)
            .reshape(block_rows, sequence_count, width)
        )
        grad_rows = (
            out_grad[micro_index].reshape(row_count, width).astype(jnp.float32) * valid[:, None]
        )
        grad_pieces = (
            (gates[:, :, None] * grad_rows[:, None, :])
            .astype(jnp.bfloat16)
            .reshape(row_count * top_count, width)
        )
        grad_out = (
            jnp.zeros((expert_count * capacity, width), jnp.bfloat16).at[slots].set(grad_pieces)
        )
        grad_arrived = lax.all_to_all(
            grad_out.reshape(axis_devices, local_experts, capacity, width),
            "ep",
            split_axis=0,
            concat_axis=0,
            tiled=True,
        )
        inner_grad = jnp.einsum(
            "secd,efd->secf", grad_arrived, w_down, preferred_element_type=jnp.float32
        )
        sigmoid_gate = jax.nn.sigmoid(gate_in)
        gate_in_grad = (
            inner_grad * up_in * sigmoid_gate * (1.0 + gate_in * (1.0 - sigmoid_gate))
        ).astype(jnp.bfloat16)
        up_in_grad = (inner_grad * active).astype(jnp.bfloat16)
        grad_gate = grad_gate + jnp.einsum(
            "secd,secf->edf", arrived, gate_in_grad, preferred_element_type=jnp.float32
        )
        grad_up = grad_up + jnp.einsum(
            "secd,secf->edf", arrived, up_in_grad, preferred_element_type=jnp.float32
        )
        grad_down = grad_down + jnp.einsum(
            "secf,secd->efd", inner, grad_arrived, preferred_element_type=jnp.float32
        )
        expert_grad = jnp.einsum(
            "secf,edf->secd", gate_in_grad, w_gate, preferred_element_type=jnp.float32
        )
        expert_grad = expert_grad + jnp.einsum(
            "secf,edf->secd", up_in_grad, w_up, preferred_element_type=jnp.float32
        )
        grad_back = lax.all_to_all(
            expert_grad, "ep", split_axis=0, concat_axis=0, tiled=True
        ).reshape(expert_count * capacity, width)
        moe_in_part = jnp.sum(grad_back[slots].reshape(row_count, top_count, width), axis=1)
        gate_part = jnp.sum(grad_rows[:, None, :] * picked_rows.astype(jnp.float32), axis=-1)
        moe_in_grad, gate_grad_rows = lax.psum((moe_in_part, gate_part), "tp")
        prob_grad = jnp.sum(picked_float * gate_grad_rows[:, :, None], axis=1)
        logit_grad = (
            probs * (prob_grad - jnp.sum(probs * prob_grad, axis=1, keepdims=True))
        ).astype(jnp.bfloat16)
        grad_router = grad_router + contract_rows(normed_mid, logit_grad)
        normed_mid_grad = moe_in_grad + contract_cols(logit_grad, full_router)
        grad_gain_moe = grad_gain_moe + jnp.sum(normed_mid_grad * middle * scale_mid, axis=0)
        scaled_mid = gain_moe * normed_mid_grad
        middle_grad = (
            grad_rows
            + scale_mid * scaled_mid
            - middle * scale_mid**3 * jnp.mean(scaled_mid * middle, axis=1, keepdims=True)
        )
        middle_low = middle_grad.astype(jnp.bfloat16)
        grad_output = grad_output + contract_rows(middle_low, attended)
        attended_grad = (
            jnp.dot(middle_low, full_output, preferred_element_type=jnp.float32)
            .astype(jnp.bfloat16)
            .reshape(head_shape)
        )
        key_back, value_back = gather_keys(key_blocks, value_blocks)
        query_grads = []
        key_grads = []
        value_grads = []
        centres = []
        for sequence in range(sequence_count):
            query_one, key_one, value_one, centre_one = attend_backward(
                query_turned[:, sequence],
                key_back[:, sequence].reshape(sequence_length, local_heads, HEAD_DIM),
                value_back[:, sequence].reshape(sequence_length, local_heads, HEAD_DIM),
                attended_grad[:, sequence],
                log_totals[sequence],
                first_place,
                lengths[micro_index, sequence],
                score_scale,
            )
            query_grads.append(query_one)
            key_grads.append(key_one)
            value_grads.append(value_one)
            centres.append(centre_one)
        key_grad_all = jnp.stack(key_grads, axis=1).reshape(
            sequence_length, sequence_count, local_width
        )
        value_grad_all = jnp.stack(value_grads, axis=1).reshape(
            sequence_length, sequence_count, local_width
        )
        key_grad, value_grad = (
            lax.psum_scatter(
                key_grad_all.astype(jnp.bfloat16), "ep", scatter_dimension=0, tiled=True
            ).astype(jnp.float32),
            lax.psum_scatter(
                value_grad_all.astype(jnp.bfloat16), "ep", scatter_dimension=0, tiled=True
            ).astype(jnp.float32),
        )
        value_grad_low = value_grad.reshape(row_count, local_width).astype(jnp.bfloat16)
        query_norm_grad = rotate_back(
            jnp.stack(query_grads, axis=1), cosine_table, sine_table
        ).reshape(row_count, local_width)
        key_norm_grad = rotate_back(key_grad.reshape(head_shape), cosine_table, sine_table).reshape(
            row_count, local_width
        )
        query_inner, key_inner = lax.psum(
            (
                jnp.sum(gain_query * query_norm_grad * query_pre, axis=1),
                jnp.sum(gain_key * key_norm_grad * key_pre, axis=1),
            ),
            "tp",
        )
        query_pre_grad = (
            query_scale * gain_query * query_norm_grad
            - query_pre * query_scale**3 * query_inner[:, None] / width
        ).astype(jnp.bfloat16)
        key_pre_grad = (
            key_scale * gain_key * key_norm_grad
            - key_pre * key_scale**3 * key_inner[:, None] / width
        ).astype(jnp.bfloat16)
        query_gain_piece = jnp.sum(query_norm_grad * query_pre * query_scale, axis=0)
        key_gain_piece = jnp.sum(key_norm_grad * key_pre * key_scale, axis=0)
        grad_query = grad_query + contract_rows(normed_in, query_pre_grad)
        grad_key = grad_key + contract_rows(normed_in, key_pre_grad)
        grad_value = grad_value + contract_rows(normed_in, value_grad_low)
        input_part = (
            contract_cols(query_pre_grad, full_query)
            + contract_cols(key_pre_grad, full_key)
            + contract_cols(value_grad_low, full_value)
        )
        query_gain_full = lax.dynamic_update_slice(
            zero_width, query_gain_piece, (hidden_index * local_width,)
        )
        key_gain_full = lax.dynamic_update_slice(
            zero_width, key_gain_piece, (hidden_index * local_width,)
        )
        normed_in_grad, query_gain_sum, key_gain_sum = (
            lax.psum(input_part.astype(jnp.bfloat16), "tp").astype(jnp.float32),
            lax.psum(query_gain_full.astype(jnp.bfloat16), "tp").astype(jnp.float32),
            lax.psum(key_gain_full.astype(jnp.bfloat16), "tp").astype(jnp.float32),
        )
        grad_gain_query = grad_gain_query + query_gain_sum
        grad_gain_key = grad_gain_key + key_gain_sum
        grad_gain_attn = grad_gain_attn + jnp.sum(normed_in_grad * hidden_in * scale_in, axis=0)
        scaled_in = gain_attn * normed_in_grad
        hidden_grad = (
            middle_grad
            + scale_in * scaled_in
            - hidden_in * scale_in**3 * jnp.mean(scaled_in * hidden_in, axis=1, keepdims=True)
        )
        input_grads.append(hidden_grad.reshape(block_rows, sequence_count, width))
    summed = (
        lax.psum_scatter(
            grad_query.astype(jnp.bfloat16), "ep", scatter_dimension=0, tiled=True
        ).astype(jnp.float32),
        lax.psum_scatter(
            grad_key.astype(jnp.bfloat16), "ep", scatter_dimension=0, tiled=True
        ).astype(jnp.float32),
        lax.psum_scatter(
            grad_value.astype(jnp.bfloat16), "ep", scatter_dimension=0, tiled=True
        ).astype(jnp.float32),
        lax.psum_scatter(
            grad_output.astype(jnp.bfloat16), "ep", scatter_dimension=0, tiled=True
        ).astype(jnp.float32),
        lax.psum_scatter(
            grad_router.astype(jnp.bfloat16), "ep", scatter_dimension=0, tiled=True
        ).astype(jnp.float32),
        lax.psum_scatter(
            grad_gain_attn.astype(jnp.bfloat16), "ep", scatter_dimension=0, tiled=True
        ).astype(jnp.float32),
        lax.psum_scatter(
            grad_gain_moe.astype(jnp.bfloat16), "ep", scatter_dimension=0, tiled=True
        ).astype(jnp.float32),
        lax.psum_scatter(
            grad_gain_query.astype(jnp.bfloat16), "ep", scatter_dimension=0, tiled=True
        ).astype(jnp.float32),
        lax.psum_scatter(
            grad_gain_key.astype(jnp.bfloat16), "ep", scatter_dimension=0, tiled=True
        ).astype(jnp.float32),
    )
    return (
        jnp.stack(outputs_list, axis=0),
        jnp.stack(input_grads, axis=0),
        summed[0],
        summed[1],
        summed[2],
        summed[3],
        summed[4],
        summed[5],
        summed[6],
        summed[7],
        summed[8],
        grad_gate,
        grad_up,
        grad_down,
    )


MESH = pl.DeviceIdType.MESH
ANYWHERE = pl.BlockSpec(memory_space=pl.ANY)
IN_VMEM = pl.BlockSpec(memory_space=pltpu.VMEM)
LANES = 128
BLOCK_BITS = ("y", "x", "z", "c")
HEAD_BITS = ("x", "z", "c", "y")
TURNS = (("z", "x", "y"), ("x", "y", "z"), ("y", "z", "x"))


def place_bits():
    ep = lax.axis_index("ep")
    tp = lax.axis_index("tp")
    return {
        "h": ep // 4,
        "z": (ep // 2) % 2,
        "x": ep % 2,
        "y": tp // 2,
        "c": tp % 2,
    }


def device_of(bits):
    return {"ep": 4 * bits["h"] + 2 * bits["z"] + bits["x"], "tp": 2 * bits["y"] + bits["c"]}


def flipped(bits, *names):
    turned = dict(bits)
    for name in names:
        turned[name] = 1 - turned[name]
    return device_of(turned)


def block_index(bits, order):
    return sum(bits[name] * (1 << k) for k, name in enumerate(order))


def held_segments(bits, gathered, order):
    run = 0
    while run < len(order) and order[run] in gathered:
        run += 1
    base, combos = 0, [0]
    for k in range(run, len(order)):
        weight = LANES << k
        if order[k] in gathered:
            combos = [v + s * weight for v in combos for s in (0, 1)]
        else:
            base = base + bits[order[k]] * weight
    return [(pl.multiple_of(base + v, LANES), LANES << run) for v in combos]


class Wires:
    def __init__(self, bits, send, recv):
        self.bits, self.send, self.recv = bits, send, recv
        self.count, self.pending = 0, []

    def start(self, source, target, *names):
        k = self.count
        self.count += 1
        copy = pltpu.make_async_remote_copy(
            src_ref=source,
            dst_ref=target,
            send_sem=self.send.at[k],
            recv_sem=self.recv.at[k],
            device_id=flipped(self.bits, *names),
            device_id_type=MESH,
        )
        copy.start()
        self.pending.append(copy)
        return copy

    def settle(self, copy):
        copy.wait()
        self.pending = [other for other in self.pending if other is not copy]

    def sent(self, copies):
        for copy in copies:
            copy.wait_send()
        self.pending = [other for other in self.pending if all(other is not c for c in copies)]

    def finish(self):
        for copy in self.pending:
            copy.wait_send()


def greet(bits, partners):
    barrier = pltpu.get_barrier_semaphore()
    for names in partners:
        pl.semaphore_signal(
            barrier, inc=1, device_id=flipped(bits, *names), device_id_type=MESH
        )
    pl.semaphore_wait(barrier, len(partners))


def receive(copies):
    for copy in copies:
        copy.wait_recv()


EP_MASKS = (("z",), ("x",), ("z", "x"), ("h",), ("h", "z"), ("h", "x"), ("h", "z", "x"))


CUBE_MASKS = tuple(
    tuple(n for k, n in enumerate("zxyc") if mask >> k & 1) for mask in range(1, 16)
)


ALL_MASKS = CUBE_MASKS + (("h",),) + tuple(("h",) + names for names in CUBE_MASKS)


def semaphores(count):
    return [pltpu.SemaphoreType.DMA((count,)), pltpu.SemaphoreType.DMA((count,))]


def spread_kernel(
    inp, wq, wk, wv, small,
    xg, wh, sm,
    local, send, recv,
):
    bits = place_bits()
    h, z, x, y, c = (bits[n] for n in "hzxyc")
    wires = Wires(bits, send, recv)
    locals_ = []

    def keep(source, target):
        copy = pltpu.make_async_copy(source, target, local.at[len(locals_)])
        copy.start()
        locals_.append(copy)

    cuts = ((0, 384), (384, 384), (768, 256), (1024, 384), (1408, 384), (1792, 256))
    x_first = [
        wires.start(
            inp.at[1 - h, y, c, :, pl.ds(lo, n)], xg.at[y, h, z, x, c, :, pl.ds(lo, n)], "h"
        )
        for lo, n in cuts
    ]
    keep(inp.at[h, y, c], xg.at[y, h, z, x, c])
    small_copies = [wires.start(small, sm.at[h, z, x], *names) for names in EP_MASKS]
    keep(small, sm.at[h, z, x])
    head_copies = []
    for m, weight in enumerate((wq, wk, wv)):
        for names in EP_MASKS:
            if "h" not in names:
                continue
            tz = 1 - z if "z" in names else z
            tx = 1 - x if "x" in names else x
            cols = pl.ds(pl.multiple_of((2 * tz + tx) * LANES, LANES), LANES)
            head_copies.append(
                wires.start(
                    weight.at[:, cols], wh.at[h, z, x, :, pl.ds(m * LANES, LANES)], *names
                )
            )
    for m, weight in enumerate((wq, wk, wv)):
        for names in EP_MASKS:
            if "h" in names:
                continue
            tz = 1 - z if "z" in names else z
            tx = 1 - x if "x" in names else x
            cols = pl.ds(pl.multiple_of((2 * tz + tx) * LANES, LANES), LANES)
            head_copies.append(
                wires.start(
                    weight.at[:, cols], wh.at[h, z, x, :, pl.ds(m * LANES, LANES)], *names
                )
            )
        own = pl.ds(pl.multiple_of((2 * z + x) * LANES, LANES), LANES)
        keep(weight.at[:, own], wh.at[h, z, x, :, pl.ds(m * LANES, LANES)])
    for copy in locals_:
        copy.wait()

    def slot(ref, gathered, lo, n):
        pick = tuple(
            slice(None) if name == "h" or name in gathered else bits[name] for name in "yhzxc"
        )
        return ref.at[pick + (slice(None), pl.ds(lo, n))]

    for ref, first in ((xg, x_first),):
        arriving = [[copy] for copy in first]
        gathered = [set() for _ in cuts]
        for stage in range(4):
            for k, (lo, n) in enumerate(cuts):
                receive(arriving[k])
                name = (TURNS[k % 3] + ("c",))[stage]
                part = slot(ref, gathered[k], lo, n)
                arriving[k] = [wires.start(part, part, name)]
                gathered[k] = gathered[k] | {name}
        for copies in arriving:
            receive(copies)
    receive(head_copies)
    receive(small_copies)
    wires.finish()


def spread_inputs(inp, wq, wk, wv, small):
    micro, rows, width = inp.shape
    cut = (micro, 2, 2, rows // 4, width)
    xg, wh, sm = pl.pallas_call(
        spread_kernel,
        out_shape=(
            jax.ShapeDtypeStruct((2, 2, 2, 2, 2, rows // 4, width), jnp.bfloat16),
            jax.ShapeDtypeStruct((2, 2, 2, wq.shape[0], 3 * LANES), jnp.bfloat16),
            jax.ShapeDtypeStruct((2, 2, 2) + small.shape, small.dtype),
        ),
        in_specs=[ANYWHERE] * 5,
        out_specs=[ANYWHERE] * 3,
        scratch_shapes=[pltpu.SemaphoreType.DMA((16,)), *semaphores(96)],
        compiler_params=pltpu.CompilerParams(has_side_effects=True),
    )(inp.reshape(cut), wq, wk, wv, small)
    return (
        xg.reshape(8 * rows, width),
        wh.reshape(width, 3 * LANES),
        sm.reshape(8, *small.shape),
    )


def row_cuts(rows):
    step = -(-rows // 96) * 16
    return [
        (lo, min(step, rows - lo), TURNS[k % 3] + ("c",))
        for k, lo in enumerate(range(0, rows, step))
    ]


def start_stage(wires, bits, order, block, whole, lead, lo, n, gathered, name):
    copies = []
    for offset, width in held_segments(bits, gathered, order):
        target = whole.at[lead + (pl.ds(lo, n), pl.ds(offset, width))]
        source = target if gathered else block.at[pl.ds(lo, n)]
        copies.append(wires.start(source, target, name))
    return copies


def add_strips(target, left, right):
    rows = target.shape[0]
    step = 32

    def strip(k, carry):
        at = pl.ds(pl.multiple_of(k * step, step), step)
        total = left[at].astype(jnp.float32) + right[at].astype(jnp.float32)
        target[at] = total.astype(target.dtype)
        return carry

    lax.fori_loop(0, rows // step, strip, 0)


class Reduction:
    def __init__(self, wires, bits, source, turns, buffers, local):
        self.wires, self.bits, self.source = wires, bits, source
        self.turns, self.buffers, self.local = turns, buffers, local
        self.order = ["y", "x", "z"]

    def start(self):
        b = self.buffers
        half = 8 * LANES
        c = self.bits["c"]
        mine = pl.ds(pl.multiple_of(c * half, half), half)
        other = pl.ds(pl.multiple_of((1 - c) * half, half), half)
        self.copies = [self.wires.start(self.source.at[:, other], b["r"][0], "c")]
        self.loaded = pltpu.make_async_copy(self.source.at[:, mine], b["a"][0], self.local)
        self.loaded.start()

    def pieces(self, name):
        k = self.order.index(name)
        count = len(self.order)
        width = LANES << k
        kept, sent = [], []
        for s in range(1 << (count - 1 - k)):
            base = s * 2 * width
            near = pl.multiple_of(base + self.bits[name] * width, LANES)
            far = pl.multiple_of(base + (1 - self.bits[name]) * width, LANES)
            kept.append((near, s * width, width))
            sent.append((far, s * width, width))
        return kept, sent

    def step(self, stage):
        b = self.buffers
        receive(self.copies)
        if stage == 1:
            self.loaded.wait()
            add_strips(b["a"][0], b["a"][0], b["r"][0])
        else:
            name = self.turns[stage - 2]
            kept, _ = self.pieces(name)
            for at, to, width in kept:
                add_strips(
                    b["a"][stage - 1].at[:, pl.ds(to, width)],
                    b["a"][stage - 2].at[:, pl.ds(at, width)],
                    b["r"][stage - 1].at[:, pl.ds(to, width)],
                )
            self.order = [n for n in self.order if n != name]
        if stage == 4:
            return
        name = self.turns[stage - 1]
        _, sent = self.pieces(name)
        self.copies = [
            self.wires.start(
                b["a"][stage - 1].at[:, pl.ds(at, width)],
                b["r"][stage].at[:, pl.ds(to, width)],
                name,
            )
            for at, to, width in sent
        ]


def reduction_buffers(count, rows):
    widths = [8 * LANES, 4 * LANES, 2 * LANES, LANES]
    shapes = []
    for width in widths:
        shapes.append(pltpu.VMEM((count, rows, width), jnp.bfloat16))
        shapes.append(pltpu.VMEM((count, rows, width), jnp.bfloat16))
    return shapes


def buffers_of(scratch, k):
    return {
        "a": [scratch[2 * s].at[k] for s in range(4)],
        "r": [scratch[2 * s + 1].at[k] for s in range(4)],
    }


STRIP = 256


def reductions(wires, bits, pool, local, sources):
    chunks = []
    for k, (source, what) in enumerate(sources):
        chunk = Reduction(wires, bits, source, TURNS[k % 3], buffers_of(pool, k), local.at[k])
        chunk.what = what
        chunks.append(chunk)
    for chunk in chunks:
        chunk.start()
    return chunks


EXPERT_ROWS = 512
STRIP_ROWS = 32
BLOCK_CUTS = ((0, 192, TURNS[0]), (192, 160, TURNS[1]), (352, 160, TURNS[2]))


def rows_dot(left, right):
    return lax.dot_general(
        left, right, (((0,), (0,)), ((), ())), preferred_element_type=jnp.float32
    )


def half_pieces(bits, order, name):
    k = order.index(name)
    width = LANES << k
    kept, sent = [], []
    for s in range(1 << (len(order) - 1 - k)):
        base = s * 2 * width
        near = pl.multiple_of(base + bits[name] * width, LANES)
        far = pl.multiple_of(base + (1 - bits[name]) * width, LANES)
        kept.append((near, s * width, width))
        sent.append((far, s * width, width))
    return kept, sent


def add_into(target, source, step=32):
    def strip(k, carry):
        at = pl.ds(pl.multiple_of(k * step, step), step)
        total = target[at].astype(jnp.float32) + source[at].astype(jnp.float32)
        target[at] = total.astype(target.dtype)
        return carry

    lax.fori_loop(0, target.shape[0] // step, strip, 0)


def experts_kernel(
    attended, wo, x_block, gain, grads_all, w_gate_in, w_up_in, w_down_in, router_in, mask_in,
    middle, gained, wh, out_part, normed_total, tiny_out, logits_own, gate_out, up_out, down_out,
    w_gate, w_up, w_down, router, mask, grad_gate, grad_up, grad_down,
    wor, squares, rows_all, grads, out, normed, inner_low, left_low, all_squares,
    a_full, b_full, du_full, gates_full, scale_full, terms,
    r0, r1, r2, r3, cross, tiny_sum, tiny_in,
    local, load, store, read, write, gather_send, gather_recv, scatter_send, scatter_recv,
    cross_send, cross_recv, tiny_sems, wo_send, wo_recv, send, recv,
):
    bits = place_bits()
    h, z, x, y, c = (bits[n] for n in "hzxyc")
    ep = 4 * h + 2 * z + x
    local_experts = w_gate.shape[0]
    width, hidden = rows_all.shape[2], w_gate.shape[2]
    expert_count = 8 * local_experts
    wires = Wires(bits, send, recv)
    [(offset, _)] = held_segments(bits, (), BLOCK_BITS)
    own_cols = pl.ds(offset, LANES)
    blocks = 4
    tile = width // 4

    def is_foreign(k):
        return ((k + 1) // 2) % 2

    def micro_of(k):
        return h + is_foreign(k) * (1 - 2 * h)

    def start_of(k):
        return pl.multiple_of((k // 2) * EXPERT_ROWS, EXPERT_ROWS)

    def remote(source, target, s_sem, r_sem, *names):
        return pltpu.make_async_remote_copy(
            src_ref=source,
            dst_ref=target,
            send_sem=s_sem,
            recv_sem=r_sem,
            device_id=flipped(bits, *names),
            device_id_type=MESH,
        )

    def gather_copies(k, stage):
        copies, index = [], 0
        for lo, n, turns in BLOCK_CUTS:
            order = turns + ("c",)
            for s in range(4):
                for seg, wide in held_segments(bits, order[:s], BLOCK_BITS):
                    if s == stage:
                        part = rows_all.at[
                            micro_of(k), pl.ds(start_of(k) + lo, n), pl.ds(seg, wide)
                        ]
                        copies.append(
                            remote(
                                part, part, gather_send.at[k, index], gather_recv.at[k, index], order[s]
                            )
                        )
                    index += 1
        return copies

    def gather_step(k, stage):
        if stage > 0:
            for copy in gather_copies(k, stage - 1):
                copy.wait_recv()
        if stage < 4:
            for copy in gather_copies(k, stage):
                copy.start()
        else:
            for s in range(4):
                for copy in gather_copies(k, s):
                    copy.wait_send()

    held = (r0, r1, r2, r3)

    def scatter_copies(k, stage):
        copies, index = [], 0
        for a, source in enumerate((normed,)):
            for lo, n, turns in BLOCK_CUTS:
                order = ["y", "x", "z"]
                at = pl.ds(lo, n)
                for s in range(4):
                    if s == 0:
                        other = pl.ds(pl.multiple_of((1 - c) * 8 * LANES, 8 * LANES), 8 * LANES)
                        pairs = [(source.at[at, other], r0.at[k, a, at])]
                        name = "c"
                    else:
                        name = turns[s - 1]
                        _, sent = half_pieces(bits, order, name)
                        pairs = [
                            (
                                held[s - 1].at[k, a, at, pl.ds(far, wide)],
                                held[s].at[k, a, at, pl.ds(to, wide)],
                            )
                            for far, to, wide in sent
                        ]
                        order = [n_ for n_ in order if n_ != name]
                    for src, dst in pairs:
                        if s == stage:
                            copies.append(
                                remote(
                                    src, dst, scatter_send.at[k, index], scatter_recv.at[k, index], name
                                )
                            )
                        index += 1
        return copies

    def scatter_add(k, stage):
        for a, source in enumerate((normed,)):
            if stage == 0:
                mine = pl.ds(pl.multiple_of(c * 8 * LANES, 8 * LANES), 8 * LANES)
                add_into(r0.at[k, a], source.at[:, mine])
                continue
            for lo, n, turns in BLOCK_CUTS:
                order = [b for b in ("y", "x", "z") if b not in turns[: stage - 1]]
                kept, _ = half_pieces(bits, order, turns[stage - 1])
                at = pl.ds(lo, n)
                for near, to, wide in kept:
                    add_into(
                        held[stage].at[k, a, at, pl.ds(to, wide)],
                        held[stage - 1].at[k, a, at, pl.ds(near, wide)],
                    )

    def cross_copies(k):
        half = k // 2
        return [
            remote(
                r3.at[k, a],
                cross.at[a, pl.ds(start_of(k), EXPERT_ROWS)],
                cross_send.at[a, half],
                cross_recv.at[a, half],
                "h",
            )
            for a in range(1)
        ]

    def scatter_step(k, stage):
        if stage > 0:
            for copy in scatter_copies(k, stage - 1):
                copy.wait()
            scatter_add(k, stage - 1)
        if stage < 4:
            for copy in scatter_copies(k, stage):
                copy.start()
        else:

            @pl.when(is_foreign(k) == 1)
            def _():
                for copy in cross_copies(k):
                    copy.start()

    def grad_read(k):
        s = k % 2
        return pltpu.make_async_copy(
            grads_all.at[:, micro_of(k), k // 2],
            grads.at[s].reshape(grads_all.shape[0], grads_all.shape[3], width),
            read.at[s],
        )

    def tiny_copy(stage):
        return remote(
            tiny_sum, tiny_in.at[stage], tiny_sems.at[0, stage], tiny_sems.at[1, stage], "cy"[stage]
        )

    def out_write(k):
        return pltpu.make_async_copy(
            out, out_part.at[micro_of(k), pl.ds(start_of(k), EXPERT_ROWS)], write
        )

    tp = 2 * y + c
    halves = (out, normed)
    [(head_offset, _)] = held_segments(bits, (), HEAD_BITS)
    own = []
    for half in (0, 1):
        at = pl.ds(half * EXPERT_ROWS, EXPERT_ROWS)
        own.append(
            pltpu.make_async_copy(
                attended.at[at], halves[half].at[:, pl.ds(head_offset, LANES)], local.at[3 * half]
            )
        )
        own[half].start()
    grad_read(0).start()
    loads = [
        pltpu.make_async_copy(source, target, load.at[n])
        for n, (source, target) in enumerate(
            (
                (router_in, router),
                (mask_in, mask),
                (w_gate_in, w_gate),
                (w_up_in, w_up),
                (w_down_in, w_down),
            )
        )
    ]
    for copy in loads:
        copy.start()
    greet(bits, ALL_MASKS)
    arriving = [[[] for _ in BLOCK_CUTS] for _ in halves]
    heads_sent = []

    def heads_stage(half, stage):
        for n, (lo, count, turns) in enumerate(BLOCK_CUTS):
            order = turns + ("c",)
            receive(arriving[half][n])
            arriving[half][n] = []
            if stage == 4:
                continue
            for seg, wide in held_segments(bits, order[:stage], HEAD_BITS):
                part = halves[half].at[pl.ds(lo, count), pl.ds(seg, wide)]
                arriving[half][n].append(wires.start(part, part, order[stage]))
            heads_sent.extend(arriving[half][n])

    for half in (0, 1):
        own[half].wait()
        heads_stage(half, 0)
    def output_row_copy(a, p):
        ty = 1 - y if p else y
        rows = pl.ds(pl.multiple_of(ty * LANES, LANES), LANES)
        cols = pl.ds(pl.multiple_of(tp * 4 * LANES, LANES), 4 * LANES)
        return pltpu.make_async_remote_copy(
            src_ref=wo.at[rows],
            dst_ref=wor.at[:, cols],
            send_sem=wo_send.at[2 * a + p],
            recv_sem=wo_recv.at[tp],
            device_id=device_of({"h": 1 - h if a else h, "z": z, "x": x, "y": ty, "c": h}),
            device_id_type=MESH,
        )

    def own_row_copy():
        rows = pl.ds(pl.multiple_of(y * LANES, LANES), LANES)
        cols = pl.ds(pl.multiple_of(tp * 4 * LANES, LANES), 4 * LANES)
        return pltpu.make_async_copy(wo.at[rows], wor.at[:, cols], local.at[1])

    for a in (0, 1):
        for p in (0, 1):
            if a == 0 and p == 0:
                pl.when(c != h)(lambda: output_row_copy(0, 0).start())
                pl.when(c == h)(lambda: own_row_copy().start())
            else:
                output_row_copy(a, p).start()
    def head_columns(tz, tx):
        return wo.at[:, pl.ds(pl.multiple_of((2 * tz + tx) * LANES, LANES), LANES)]

    head_copies = [
        wires.start(
            head_columns(1 - z if "z" in names else z, 1 - x if "x" in names else x),
            wh.at[h, z, x],
            *names,
        )
        for names in EP_MASKS
    ]
    own_head = pltpu.make_async_copy(head_columns(z, x), wh.at[h, z, x], local.at[2])
    own_head.start()
    for stage in (1, 2, 3):
        for half in (0, 1):
            heads_stage(half, stage)
    for source in range(4):
        sy, sc = source // 2, source % 2

        def arrived(source=source):
            pltpu.make_async_remote_copy(
                src_ref=wo.at[pl.ds(0, LANES)],
                dst_ref=wor.at[:, pl.ds(source * 4 * LANES, 4 * LANES)],
                send_sem=wo_send.at[0],
                recv_sem=wo_recv.at[source],
                device_id=flipped(bits, "h"),
                device_id_type=MESH,
            ).wait_recv()

        pl.when(jnp.logical_or(c != h, tp != source))(arrived)
    pl.when(c == h)(lambda: own_row_copy().wait())
    for a in (0, 1):
        for p in (0, 1):
            if a == 0 and p == 0:
                pl.when(c != h)(lambda: output_row_copy(0, 0).wait_send())
            else:
                output_row_copy(a, p).wait_send()
    crossing, square_copies = [], []

    def project(half):
        heads_stage(half, 4)
        at = pl.ds(half * EXPERT_ROWS, EXPERT_ROWS)
        rows_now = x_block[at].astype(jnp.float32) + contract_cols(halves[half][...], wor[...])
        middle[at] = rows_now
        low = (rows_now * gain[0:1]).astype(jnp.bfloat16)
        gained[at] = low
        rows_all[h, at, own_cols] = low
        lines = row_lines(rows_now * rows_now)
        squares[half] = jnp.concatenate([lines, lines], axis=0)
        all_squares[half, h, c, z, x, y] = squares[half]

    def announce(half):
        at = pl.ds(half * EXPERT_ROWS, EXPERT_ROWS)
        part = rows_all.at[h, at, own_cols]
        square_copies.append(
            [
                wires.start(squares.at[half], all_squares.at[half, h, c, z, x, y], *names)
                for names in CUBE_MASKS
            ]
        )
        crossing.append(wires.start(part, part, "h"))

    project(0)
    gather_step(0, 0)
    announce(0)
    project(1)
    gather_step(0, 1)
    announce(1)
    gather_step(0, 2)
    for copies in square_copies:
        receive(copies)
    square_cross = wires.start(all_squares.at[:, h], all_squares.at[:, h], "h")
    gather_step(0, 3)
    crossing[0].wait_recv()
    gather_step(1, 0)
    gather_step(0, 4)
    gather_step(1, 1)
    receive(head_copies)
    own_head.wait()
    wires.sent(heads_sent)
    grad_gate[...] = jnp.zeros_like(grad_gate)
    grad_up[...] = jnp.zeros_like(grad_up)
    grad_down[...] = jnp.zeros_like(grad_down)
    for copy in loads:
        copy.wait()

    @pl.loop(0, blocks)
    def _(k):
        slot = k % 2
        micro, first = micro_of(k), start_of(k)
        at = pl.ds(first, EXPERT_ROWS)
        rows = rows_all.at[micro, at]
        grad = grads.at[slot]
        more, two_more, before = k < blocks - 1, k < blocks - 2, k > 0
        last = k == blocks - 1

        def when(flag, step, which, stage):
            pl.when(flag)(lambda: step(which, stage))

        pl.when(more)(lambda: grad_read(k + 1).start())
        pl.when(k == 1)(square_cross.wait_recv)
        when(more, gather_step, k + 1, 2)
        grad_read(k).wait()

        sums = jnp.sum(all_squares[k // 2, micro].reshape(16, 8, LANES), axis=0)
        scales = lax.rsqrt(sums / width + EPSILON)
        for s in range(4):
            scale_full[pl.ds(s * LANES, LANES)] = jnp.broadcast_to(
                scales[s : s + 1], (LANES, LANES)
            ).T
        logits = scale_full[...] * jnp.dot(
            rows[...], router[...], preferred_element_type=jnp.float32
        )
        lane = lax.broadcasted_iota(jnp.int32, logits.shape, 1)

        @pl.when(is_foreign(k) == 0)
        def _():
            logits_own[at] = jnp.where(lane == expert_count, scale_full[...], logits)

        shown = jnp.where(lane < expert_count, logits, NEGATIVE)
        weights = jnp.exp(shown - jnp.max(shown, axis=1, keepdims=True))
        gates = weights / jnp.sum(weights, axis=1, keepdims=True)
        gates = gates * mask[micro, at].astype(jnp.float32)
        for e in range(local_experts):
            gate = jnp.sum(
                jnp.where(lane == ep * local_experts + e, gates, 0.0), axis=1, keepdims=True
            )
            gates_full[e] = jnp.broadcast_to(gate, logits.shape)
        for e in range(local_experts):
            a_full[...] = jnp.dot(rows[...], w_gate[e], preferred_element_type=jnp.float32)
            b_full[...] = jnp.dot(rows[...], w_up[e], preferred_element_type=jnp.float32)
            du_full[...] = contract_cols(grad[...], w_down[e])

            @pl.loop(0, EXPERT_ROWS // STRIP_ROWS, unroll=2)
            def _(n):
                part = pl.ds(pl.multiple_of(n * STRIP_ROWS, STRIP_ROWS), STRIP_ROWS)
                scale, gate = scale_full[part], gates_full[e, part]
                for lo in range(0, hidden, LANES):
                    cols = pl.ds(lo, LANES)
                    a = scale * a_full[part, cols]
                    b = scale * b_full[part, cols]
                    du = du_full[part, cols]
                    sigma = 0.5 * jnp.tanh(0.5 * a) + 0.5
                    active = a * sigma
                    u = active * b
                    inner_low[e, part, cols] = (u * gate).astype(jnp.bfloat16)
                    terms[part, pl.ds(e * hidden + lo, LANES)] = (u * du).astype(jnp.bfloat16)
                    du = du * gate
                    da = du * b * (sigma + active * (1.0 - sigma))
                    db = du * active
                    terms[part, pl.ds((local_experts + e) * hidden + lo, LANES)] = (
                        da * a + db * b
                    ).astype(jnp.bfloat16)
                    left_low[2 * e, part, cols] = (da * scale).astype(jnp.bfloat16)
                    left_low[2 * e + 1, part, cols] = (db * scale).astype(jnp.bfloat16)

            if e == 0:
                when(before, scatter_step, k - 1, 2)
                when(more, gather_step, k + 1, 3)
        shape = (8, 2 * local_experts * hidden)
        line = lax.broadcasted_iota(jnp.int32, shape, 0)
        owner = jnp.minimum(lax.broadcasted_iota(jnp.int32, shape, 1) // hidden, local_experts)
        tiny_sum[micro, :, at] = contract_cols((line == owner).astype(jnp.bfloat16), terms[...])
        pl.when(last)(lambda: tiny_copy(0).start())
        when(before, scatter_step, k - 1, 3)

        @pl.loop(0, 4)
        def _(t):
            cols = pl.ds(pl.multiple_of(t * tile, tile), tile)
            total = jnp.zeros((EXPERT_ROWS, tile), jnp.float32)
            for e in range(local_experts):
                total += contract_cols(left_low[2 * e], w_gate[e, cols])
                total += contract_cols(left_low[2 * e + 1], w_up[e, cols])
            normed[:, cols] = total.astype(jnp.bfloat16)

        scatter_step(k, 0)

        @pl.when(k == 0)
        def _():
            crossing[1].wait_recv()

        when(two_more, gather_step, k + 2, 0)
        pl.when(before)(lambda: out_write(k - 1).wait())

        @pl.loop(0, 4)
        def _(t):
            cols = pl.ds(pl.multiple_of(t * tile, tile), tile)
            total = jnp.dot(inner_low[0], w_down[0, :, cols], preferred_element_type=jnp.float32)
            for e in range(1, local_experts):
                total += jnp.dot(
                    inner_low[e], w_down[e, :, cols], preferred_element_type=jnp.float32
                )
            out[:, cols] = total.astype(jnp.bfloat16)

        when(before, scatter_step, k - 1, 4)

        @pl.when(is_foreign(k) == 0)
        def _():
            total = out[:, own_cols].astype(jnp.float32) + middle[at]
            out[:, own_cols] = total.astype(jnp.bfloat16)

        out_write(k).start()

        @pl.when(last)
        def _():
            tiny_copy(0).wait()
            tiny_sum[...] += tiny_in[0]
            tiny_copy(1).start()

        def add_grads(lo, hi):
            @pl.loop(lo, hi)
            def _(t):
                cols = pl.ds(pl.multiple_of(t * tile, tile), tile)
                part = rows[:, cols]
                grad_part = grad[:, cols]
                for e in range(local_experts):
                    grad_gate[e, cols] += rows_dot(part, left_low[2 * e])
                    grad_up[e, cols] += rows_dot(part, left_low[2 * e + 1])
                    grad_down[e, :, cols] += rows_dot(inner_low[e], grad_part)

        add_grads(0, 2)
        scatter_step(k, 1)
        when(more, gather_step, k + 1, 4)
        when(two_more, gather_step, k + 2, 1)
        add_grads(2, 4)

    stores = [
        pltpu.make_async_copy(source, target, store.at[n])
        for n, (source, target) in enumerate(
            ((grad_gate, gate_out), (grad_up, up_out), (grad_down, down_out))
        )
    ]
    for copy in stores:
        copy.start()
    tiny_copy(1).wait()
    tiny_sum[...] += tiny_in[1]
    slot = tiny_out.at[h, z, x]
    slot[...] = tiny_sum[h]
    tiny_copies = [
        wires.start(tiny_sum.at[1 - h if "h" in names else h], slot, *names)
        for names in EP_MASKS
    ]
    scatter_step(blocks - 1, 2)
    scatter_step(blocks - 1, 3)
    scatter_step(blocks - 1, 4)
    for k in (1, 2):
        for copy in cross_copies(k):
            copy.wait()
    for half, k in ((0, 0), (1, 3)):
        at = pl.ds(half * EXPERT_ROWS, EXPERT_ROWS)
        normed_total[at] = r3[k, 0].astype(jnp.float32) + cross[0, at].astype(jnp.float32)
    out_write(blocks - 1).wait()
    for copy in stores:
        copy.wait()
    receive(tiny_copies)
    wires.finish()


def run_experts(
    attended, wo, x_block, gain, grads_all, w_gate, w_up, w_down, router, mask, collective_id
):
    f32, bf16 = jnp.float32, jnp.bfloat16
    rows = attended.shape[0]
    width = grads_all.shape[-1]
    hidden = w_gate.shape[2]
    local_experts = w_gate.shape[0]
    part = (EXPERT_ROWS, width)
    return pl.pallas_call(
        experts_kernel,
        out_shape=(
            jax.ShapeDtypeStruct((rows, LANES), f32),
            jax.ShapeDtypeStruct((rows, LANES), bf16),
            jax.ShapeDtypeStruct((2, 2, 2, wo.shape[0], LANES), bf16),
            jax.ShapeDtypeStruct((2, rows, width), bf16),
            jax.ShapeDtypeStruct((rows, LANES), f32),
            jax.ShapeDtypeStruct((2, 2, 2, 8, rows), f32),
            jax.ShapeDtypeStruct((rows, LANES), f32),
            jax.ShapeDtypeStruct(w_gate.shape, f32),
            jax.ShapeDtypeStruct(w_up.shape, f32),
            jax.ShapeDtypeStruct(w_down.shape, f32),
        ),
        in_specs=[ANYWHERE] * 2 + [IN_VMEM] * 2 + [ANYWHERE] * 6,
        out_specs=[IN_VMEM] * 2 + [ANYWHERE] * 2 + [IN_VMEM] * 3 + [ANYWHERE] * 3,
        scratch_shapes=[
            *[pltpu.VMEM(w.shape, bf16) for w in (w_gate, w_up, w_down)],
            pltpu.VMEM(router.shape, bf16),
            pltpu.VMEM(mask.shape, bf16),
            *[pltpu.VMEM(w.shape, f32) for w in (w_gate, w_up, w_down)],
            pltpu.VMEM((LANES, width), bf16),
            pltpu.VMEM((2, 8, LANES), f32),
            pltpu.VMEM((2, rows, width), bf16),
            pltpu.VMEM((2,) + part, bf16),
            pltpu.VMEM(part, bf16),
            pltpu.VMEM(part, bf16),
            pltpu.VMEM((local_experts, EXPERT_ROWS, hidden), bf16),
            pltpu.VMEM((2 * local_experts, EXPERT_ROWS, hidden), bf16),
            pltpu.VMEM((2, 2, 2, 2, 2, 2, 8, LANES), f32),
            *[pltpu.VMEM((EXPERT_ROWS, hidden), f32)] * 3,
            pltpu.VMEM((local_experts, EXPERT_ROWS, LANES), f32),
            pltpu.VMEM((EXPERT_ROWS, LANES), f32),
            pltpu.VMEM((EXPERT_ROWS, 2 * local_experts * hidden), bf16),
            *[pltpu.VMEM((4, 1, EXPERT_ROWS, w * LANES), bf16) for w in (8, 4, 2, 1)],
            pltpu.VMEM((1, rows, LANES), bf16),
            pltpu.VMEM((2, 8, rows), f32),
            pltpu.VMEM((2, 2, 8, rows), f32),
            pltpu.SemaphoreType.DMA((4,)),
            pltpu.SemaphoreType.DMA((5,)),
            pltpu.SemaphoreType.DMA((3,)),
            pltpu.SemaphoreType.DMA((2,)),
            pltpu.SemaphoreType.DMA(()),
            *[pltpu.SemaphoreType.DMA((4, 18))] * 2,
            *[pltpu.SemaphoreType.DMA((4, 24))] * 2,
            *[pltpu.SemaphoreType.DMA((2, 2))] * 2,
            pltpu.SemaphoreType.DMA((2, 2)),
            *semaphores(4),
            *semaphores(112),
        ],
        compiler_params=pltpu.CompilerParams(
            collective_id=collective_id,
            has_side_effects=True,
            vmem_limit_bytes=60 * 2**20,
        ),
    )(attended, wo, x_block, gain, grads_all, w_gate, w_up, w_down, router, mask)


def spread_lines(lines, target):
    for n in range(lines.shape[0]):
        target[pl.ds(n * LANES, LANES)] = jnp.broadcast_to(lines[n : n + 1], (LANES, LANES)).T


def row_lines(values):
    return jnp.concatenate(
        [
            jnp.sum(values[n * LANES : (n + 1) * LANES].T, axis=0, keepdims=True)
            for n in range(values.shape[0] // LANES)
        ],
        axis=0,
    )


def masked_softmax(queries, keys, valid, score_scale):
    count = queries.shape[0]
    scores = contract_cols(queries, keys) * score_scale
    line = lax.broadcasted_iota(jnp.int32, (count, count), 0)
    lane = lax.broadcasted_iota(jnp.int32, (count, count), 1)
    scores = jnp.where(jnp.logical_and(lane <= line, valid > 0.5), scores, NEGATIVE)
    weights = jnp.exp(scores - jnp.max(scores, axis=1, keepdims=True))
    return weights / jnp.sum(weights, axis=1, keepdims=True)


def attend_kernel(
    width, query_pre, key_pre, values, tables, key_valid, gains,
    queries, keys, attended, scales,
    squares, parts, column, send, recv,
):
    bits = place_bits()
    rank = 8 * bits["z"] + 4 * bits["x"] + 2 * bits["y"] + bits["c"]
    wires = Wires(bits, send, recv)
    rows = query_pre.shape[0]
    count = rows // 2
    for n, pre in enumerate((query_pre, key_pre)):
        squares[n] = row_lines(pre[...] * pre[...])
    greet(bits, CUBE_MASKS)
    copies = [wires.start(squares, parts.at[rank], *names) for names in CUBE_MASKS]
    parts[rank] = squares[...]
    receive(copies)
    scales[...] = lax.rsqrt(jnp.sum(parts[...], axis=0) / width + EPSILON)
    for n, (pre, target) in enumerate(((query_pre, queries), (key_pre, keys))):
        spread_lines(scales[n], column)
        for s in (0, 1):
            at = pl.ds(s * count, count)
            normed = pre[at] * column[at] * gains[n : n + 1]
            turned = normed * tables[0] + pltpu.roll(normed, HEAD_DIM // 2, 1) * tables[1]
            target[at] = turned.astype(jnp.bfloat16)
    for s in (0, 1):
        at = pl.ds(s * count, count)
        probability = masked_softmax(
            queries[at], keys[at], key_valid[s : s + 1], HEAD_DIM ** (-0.5)
        )
        attended[at] = jnp.dot(
            probability.astype(jnp.bfloat16), values[at], preferred_element_type=jnp.float32
        ).astype(jnp.bfloat16)
    wires.finish()


def attend(query_pre, key_pre, values, tables, key_valid, gains, width, collective_id):
    rows = query_pre.shape[0]
    column = jax.ShapeDtypeStruct((rows, LANES), jnp.bfloat16)
    lines = (2, rows // LANES, LANES)

    def kernel(*refs):
        attend_kernel(width, *refs)

    return pl.pallas_call(
        kernel,
        out_shape=(column, column, column, jax.ShapeDtypeStruct(lines, jnp.float32)),
        in_specs=[IN_VMEM] * 6,
        out_specs=[IN_VMEM] * 4,
        scratch_shapes=[
            pltpu.VMEM(lines, jnp.float32),
            pltpu.VMEM((16,) + lines, jnp.float32),
            pltpu.VMEM((rows, LANES), jnp.float32),
            *semaphores(16),
        ],
        compiler_params=pltpu.CompilerParams(
            collective_id=collective_id, has_side_effects=True, vmem_limit_bytes=32 * 2**20
        ),
    )(query_pre, key_pre, values, tables, key_valid, gains)


def attend_sequence_back(queries, keys, values, grads, valid, score_scale):
    probability = masked_softmax(queries, keys, valid, score_scale)
    prob_grad = contract_cols(grads, values)
    centre = jnp.sum(probability * prob_grad, axis=1, keepdims=True)
    score_grad = (probability * (prob_grad - centre)).astype(jnp.bfloat16)
    query_grad = jnp.dot(score_grad, keys, preferred_element_type=jnp.float32) * score_scale
    key_grad = rows_dot(score_grad, queries) * score_scale
    value_grad = rows_dot(probability.astype(jnp.bfloat16), grads)
    return query_grad, key_grad, value_grad


def turn_back(values, cosine, sine_signed):
    return values * cosine - pltpu.roll(values, HEAD_DIM // 2, 1) * sine_signed


def backward_kernel(
    low, out_part, normed_in, heads_in, head_output_in,
    middle_grad, queries, keys, values, attended, query_pre, key_pre,
    x_block, row_values, tables, key_valid, gains, pack_in,
    arrived, out_rows, grad_rows, packs,
    low_all, normed, heads, head_output, query_scale, key_scale, scale_in, row_valid, part, pieces, left, query_norm, key_norm, inner, pack,
    out_block, grad_block, squares, square_parts, terms, term_parts, cross,
    *scratch,
):
    out_pool, part_pool = scratch[:8], scratch[8:16]
    out_local, part_local, load, own_piece, send, recv = scratch[16:]
    bits = place_bits()
    h, z, x, y, c = (bits[n] for n in "hzxyc")
    ep = 4 * h + 2 * z + x
    rows, width = low_all.shape
    count = rows // 2
    score_scale = HEAD_DIM ** (-0.5)
    f32, bf16 = jnp.float32, jnp.bfloat16
    wires = Wires(bits, send, recv)
    rank = 8 * z + 4 * x + 2 * y + c
    [(offset, _)] = held_segments(bits, (), BLOCK_BITS)
    own_cols = pl.ds(offset, LANES)

    own = pltpu.make_async_copy(low, low_all.at[:, own_cols], load.at[0])
    own.start()
    loads = [
        pltpu.make_async_copy(heads_in, heads, load.at[1]),
        pltpu.make_async_copy(normed_in, normed, load.at[2]),
        pltpu.make_async_copy(head_output_in, head_output, load.at[3]),
    ]
    for copy in loads:
        copy.start()
    greet(bits, [*CUBE_MASKS, *[names for names in EP_MASKS if "h" in names]])

    cuts = row_cuts(rows)
    arriving = [[] for _ in cuts]
    gathered = [()] * len(cuts)

    def low_stage(stage):
        for k, (lo, n, turns) in enumerate(cuts):
            receive(arriving[k])
            arriving[k] = start_stage(
                wires, bits, BLOCK_BITS, low, low_all, (), lo, n, gathered[k], turns[stage]
            )
            gathered[k] = gathered[k] + (turns[stage],)

    low_stage(0)
    outs = reductions(
        wires,
        bits,
        out_pool,
        out_local,
        [
            (out_part.at[h if side == 0 else 1 - h, pl.ds(lo, STRIP)], (side, lo))
            for side in (1, 0)
            for lo in range(0, rows, STRIP)
        ],
    )

    def out_stage(stage):
        for chunk in outs:
            chunk.step(stage)
            side, lo = chunk.what
            if stage == 4 and side == 1:
                chunk.copies = [
                    wires.start(chunk.buffers["a"][3], cross.at[pl.ds(lo, STRIP)], "h")
                ]

    own.wait()
    low_stage(1)
    for n, target in enumerate((query_scale, key_scale, scale_in, row_valid)):
        spread_lines(row_values[n], target)
    low_stage(2)
    out_stage(1)
    low_stage(3)
    for copies in arriving:
        receive(copies)
    for copy in loads:
        copy.wait()

    half = HEAD_DIM
    for s in (0, 1):
        at = pl.ds(s * count, count)
        attended_grad = jnp.dot(
            low_all[at], head_output[...], preferred_element_type=f32
        ).astype(bf16)
        query_grad, key_grad, value_grad = attend_sequence_back(
            queries[at], keys[at], values[at], attended_grad, key_valid[s : s + 1], score_scale
        )
        query_norm[at] = turn_back(query_grad, tables[0], tables[1])
        key_norm[at] = turn_back(key_grad, tables[0], tables[1])
        left[at, 2 * half :] = value_grad.astype(bf16)
        lines = pl.ds(s * (count // LANES), count // LANES)
        squares[0, lines] = row_lines(gains[0:1] * query_norm[at] * query_pre[at])
        squares[1, lines] = row_lines(gains[1:2] * key_norm[at] * key_pre[at])
    inner_copies = [wires.start(squares, square_parts.at[rank], *names) for names in CUBE_MASKS]
    square_parts[rank] = squares[...]

    piece_copies = []

    own_head = pl.ds(pl.multiple_of((2 * z + x) * half, half), half)
    own_pieces = []

    def send_pieces(m):
        cols = pl.ds(m * half, half)
        mine = pltpu.make_async_copy(
            pieces.at[ep, :, cols], arrived.at[h, m, :, own_head], own_piece.at[m]
        )
        mine.start()
        own_pieces.append(mine)
        for names in sorted(EP_MASKS, key=lambda names: "h" not in names):
            to = [1 - bits[n] if n in names else bits[n] for n in "hzx"]
            piece_copies.append(
                wires.start(
                    pieces.at[4 * to[0] + 2 * to[1] + to[2], :, cols],
                    arrived.at[h, m, :, own_head],
                    *names,
                )
            )

    def add_pieces(source, right, columns):
        rows_of = pieces.shape[1]

        @pl.loop(0, 8)
        def _(n):
            at = pl.ds(pl.multiple_of(n * rows_of, rows_of), rows_of)
            pieces[n, :, columns] = rows_dot(source[:, at], right).astype(bf16)

    add_pieces(low_all, attended[...], pl.ds(3 * half, half))
    send_pieces(3)
    add_pieces(normed, left[:, 2 * half :], pl.ds(2 * half, half))
    send_pieces(2)
    out_stage(2)
    receive(inner_copies)
    totals = jnp.sum(square_parts[...], axis=0)
    for n, (pre, norm, scale) in enumerate(
        ((query_pre, query_norm, query_scale), (key_pre, key_norm, key_scale))
    ):
        spread_lines(totals[n], inner)
        value = scale[...]
        left[:, pl.ds(n * half, half)] = (
            value * gains[n : n + 1] * norm[...]
            - pre[...] * value * value * value * inner[...] / width
        ).astype(bf16)
        pack[pl.ds(16 + 2 + n, 1)] = jnp.sum(norm[...] * pre[...] * value, axis=0, keepdims=True)
    terms[...] = row_lines(
        left[:, :half].astype(f32) * query_pre[...]
        + left[:, half : 2 * half].astype(f32) * key_pre[...]
        + left[:, 2 * half :].astype(f32) * values[...].astype(f32)
    )
    term_copies = [wires.start(terms, term_parts.at[rank], *names) for names in CUBE_MASKS]
    term_parts[rank] = terms[...]

    tile = 512

    @pl.loop(0, width // tile)
    def _(t):
        at = pl.ds(pl.multiple_of(t * tile, tile), tile)
        part[:, at] = contract_cols(left[...], heads[at]).astype(bf16)

    sums = reductions(
        wires, bits, part_pool, part_local,
        [(part.at[pl.ds(lo, STRIP)], lo) for lo in range(0, rows, STRIP)],
    )
    add_pieces(normed, left[:, : 2 * half], pl.ds(0, 2 * half))
    send_pieces(0)
    send_pieces(1)
    for chunk in sums:
        chunk.step(1)
    out_stage(3)
    for chunk in sums:
        chunk.step(2)
    out_stage(4)
    for chunk in sums:
        chunk.step(3)

    seg = rows // 16
    first, own_rows = [], []

    def send_rows(block, whole):
        def rows_for(owner):
            return block.at[:, pl.ds(pl.multiple_of(owner * seg, seg), seg)]

        target = whole.at[h, :, :, own_cols]
        mine = pltpu.make_async_copy(rows_for(ep), target, load.at[1 + len(own_rows)])
        mine.start()
        own_rows.append(mine)
        for names in sorted(EP_MASKS, key=lambda names: "h" not in names):
            to = [1 - bits[n] if n in names else bits[n] for n in "hzx"]
            first.append(wires.start(rows_for(4 * to[0] + 2 * to[1] + to[2]), target, *names))

    for chunk in outs:
        side, lo = chunk.what
        if side == 1:
            receive(chunk.copies)
    for chunk in outs:
        side, lo = chunk.what
        if side == 0:
            at = pl.ds(lo, STRIP)
            total = chunk.buffers["a"][3][...].astype(f32) + cross[at].astype(f32)
            out_block[lo // count, pl.ds(lo % count, STRIP)] = (total * row_valid[at]).astype(bf16)
    send_rows(out_block, out_rows)
    receive(term_copies)
    spread_lines(jnp.sum(term_parts[...], axis=0), inner)
    for chunk in sums:
        chunk.step(4)
    for chunk in sums:
        lo = chunk.what
        at = pl.ds(lo, STRIP)
        normed_grad = chunk.buffers["a"][3][...].astype(f32)
        scale, own_x = scale_in[at], x_block[at].astype(f32)
        grad_block[lo // count, pl.ds(lo % count, STRIP)] = (
            middle_grad[at]
            + scale * gains[2:3] * normed_grad
            - own_x * (scale * scale * inner[at] / width)
        ).astype(bf16)
        query_norm[at] = normed_grad * own_x * scale
    send_rows(grad_block, grad_rows)
    pack[pl.ds(0, 16)] = pack_in[pl.ds(0, 16)]
    pack[pl.ds(16, 1)] = jnp.sum(query_norm[...], axis=0, keepdims=True)
    pack[pl.ds(17, 1)] = pack_in[pl.ds(17, 1)]
    pack[pl.ds(20, 4)] = jnp.zeros((4, LANES), f32)
    packs[h, :, own_cols] = pack[...]
    for names in EP_MASKS:
        first.append(wires.start(pack, packs.at[h, :, own_cols], *names))
    receive(first)
    for copy in own_rows:
        copy.wait()
    gathered = ("z", "x")
    for name in "yc":
        copies = []
        for at, wide in held_segments(bits, gathered, BLOCK_BITS):
            cols = pl.ds(at, wide)
            for segment in (
                out_rows.at[:, :, :, cols], grad_rows.at[:, :, :, cols], packs.at[:, :, cols]
            ):
                copies.append(wires.start(segment, segment, name))
        receive(copies)
        gathered += (name,)
    receive(piece_copies)
    for copy in own_pieces:
        copy.wait()
    wires.finish()


def run_backward(low, out_part, normed_in, heads, head_output, vectors, collective_id):
    f32, bf16 = jnp.float32, jnp.bfloat16
    rows, width = normed_in.shape
    chunks = rows // STRIP
    column = (rows, LANES)
    lines = (rows // LANES, LANES)
    ep_count = 8
    return pl.pallas_call(
        backward_kernel,
        out_shape=(
            jax.ShapeDtypeStruct((2, 4, width // ep_count, 4 * LANES), bf16),
            jax.ShapeDtypeStruct((2, 2, rows // 16, width), bf16),
            jax.ShapeDtypeStruct((2, 2, rows // 16, width), bf16),
            jax.ShapeDtypeStruct((2, 24, width), f32),
        ),
        in_specs=[ANYWHERE] * 5 + [IN_VMEM] * len(vectors),
        out_specs=[ANYWHERE] * 3 + [IN_VMEM],
        scratch_shapes=[
            pltpu.VMEM((rows, width), bf16),
            pltpu.VMEM((rows, width), bf16),
            pltpu.VMEM(heads.shape, bf16),
            pltpu.VMEM(head_output.shape, bf16),
            *[pltpu.VMEM(column, f32)] * 4,
            pltpu.VMEM((rows, width), bf16),
            pltpu.VMEM((ep_count, width // ep_count, 4 * LANES), bf16),
            pltpu.VMEM((rows, 3 * LANES), bf16),
            pltpu.VMEM(column, f32),
            pltpu.VMEM(column, f32),
            pltpu.VMEM(column, f32),
            pltpu.VMEM((24, LANES), f32),
            pltpu.VMEM((2, rows // 2, LANES), bf16),
            pltpu.VMEM((2, rows // 2, LANES), bf16),
            pltpu.VMEM((2,) + lines, f32),
            pltpu.VMEM((16, 2) + lines, f32),
            pltpu.VMEM(lines, f32),
            pltpu.VMEM((16,) + lines, f32),
            pltpu.VMEM(column, bf16),
            *reduction_buffers(2 * chunks, STRIP),
            *reduction_buffers(chunks, STRIP),
            pltpu.SemaphoreType.DMA((2 * chunks,)),
            pltpu.SemaphoreType.DMA((chunks,)),
            pltpu.SemaphoreType.DMA((5,)),
            pltpu.SemaphoreType.DMA((4,)),
            *semaphores(288),
        ],
        compiler_params=pltpu.CompilerParams(
            collective_id=collective_id,
            has_side_effects=True,
            vmem_limit_bytes=60 * 2**20,
        ),
    )(low, out_part, normed_in, heads, head_output, *vectors)


def column_block(values, index, width=LANES):
    return lax.dynamic_slice_in_dim(values, index * width, width, axis=-1)


def as_tiles(values):
    return values.reshape(values.shape[:-1] + (values.shape[-1] // LANES, LANES))


def cube_shards(
    inputs,
    lengths,
    routes,
    w_query,
    w_key,
    w_value,
    w_output,
    w_router,
    attn_gain,
    moe_gain,
    query_gain,
    key_gain,
    w_gate,
    w_up,
    w_down,
    out_grad,
):
    f32, bf16 = jnp.float32, jnp.bfloat16
    micro_count, block_rows, sequence_count, width = inputs.shape
    ep_index = lax.axis_index("ep")
    ep_count = lax.axis_size("ep")
    local_experts = w_gate.shape[0]
    hidden = w_gate.shape[2]
    expert_count = local_experts * ep_count
    rows_dev = block_rows * sequence_count
    sequence_length = block_rows * ep_count
    rows = rows_dev * ep_count
    bits = place_bits()
    micro = bits["h"]
    block = block_index(bits, BLOCK_BITS)
    head = block_index(bits, HEAD_BITS)

    named = routes.transpose(0, 2, 1, 3).reshape(micro_count * rows_dev, -1)
    expert_numbers = jnp.arange(expert_count, dtype=jnp.int32)
    mask_own = jnp.any(named[:, :, None] == expert_numbers, axis=1).astype(bf16)
    small = jnp.concatenate(
        [
            w_router.T,
            jnp.concatenate([attn_gain, moe_gain, query_gain, key_gain]).reshape(4, -1),
            mask_own.T,
            jnp.zeros((40 - 4 - 2 * expert_count, w_router.shape[0]), bf16),
        ],
        axis=0,
    )
    local_place = ep_index * block_rows + jnp.arange(block_rows, dtype=jnp.int32)
    quarter = block_rows // lax.axis_size("tp")
    tp_index = lax.axis_index("tp")
    grad_quarter = lax.dynamic_slice_in_dim(out_grad, tp_index * quarter, quarter, axis=1)
    place_quarter = lax.dynamic_slice_in_dim(local_place, tp_index * quarter, quarter)
    valid_quarter = (place_quarter[None, :, None] < lengths[:, None, :]).astype(bf16)
    grad_quarter = (grad_quarter * valid_quarter[..., None]).transpose(0, 2, 1, 3)
    g_all = lax.all_gather(grad_quarter, ("ep", "tp"))
    x_all, w_heads, small_all = spread_inputs(
        inputs.transpose(0, 2, 1, 3).reshape(micro_count, rows_dev, width),
        w_query,
        w_key,
        w_value,
        small,
    )
    router = small_all[:, :expert_count].transpose(0, 2, 1).reshape(width, expert_count)
    gains = small_all[:, expert_count : expert_count + 4].transpose(1, 0, 2).reshape(4, width)
    gains = gains.astype(f32)
    gain_attn = gains[0]
    gain_moe = column_block(gains[1], block)
    gain_query = column_block(gains[2], head)
    gain_key = column_block(gains[3], head)
    mask = small_all[:, expert_count + 4 : 2 * expert_count + 4]
    mask = mask.reshape(ep_count, expert_count, micro_count, sequence_count, block_rows)
    mask = mask.transpose(2, 3, 0, 4, 1).reshape(micro_count * rows, expert_count).astype(f32)
    lengths_own = lax.dynamic_index_in_dim(lengths, micro, keepdims=False)

    x_float = x_all.astype(f32)
    scale_in = row_scale(x_float)
    normed_in = lax.optimization_barrier((x_float * scale_in * gain_attn).astype(bf16))
    projected = jnp.dot(normed_in, w_heads, preferred_element_type=f32)
    query_pre = projected[:, :LANES]
    key_pre = projected[:, LANES : 2 * LANES]
    value_rows = projected[:, 2 * LANES :].astype(bf16)
    places = np.arange(sequence_length, dtype=np.float32)
    inverse = np.float32(THETA_BASE) ** (
        -np.arange(HEAD_DIM // 2, dtype=np.float32) * np.float32(2.0 / HEAD_DIM)
    )
    angles = places[:, None] * inverse[None, :]
    sines = np.sin(angles)
    tables = jnp.asarray(
        np.stack(
            [
                np.concatenate([np.cos(angles)] * 2, axis=1),
                np.concatenate([-sines, sines], axis=1),
            ]
        )
    )
    valid_rows = (jnp.arange(sequence_length) < lengths_own[:, None]).astype(f32)
    gains_block = jnp.stack([gain_query, gain_key, column_block(gain_attn, block)])
    queries, keys, attended, scales = attend(
        query_pre, key_pre, value_rows, tables, valid_rows, gains_block, width, 1
    )
    x_block = column_block(x_all, block)

    pad = ((0, 0), (0, LANES - expert_count))
    mask = jnp.pad(mask, pad).astype(bf16).reshape(micro_count, rows, LANES)
    (
        middle,
        middle_gained,
        w_head_output,
        out_part,
        normed_grad_block,
        tiny_all,
        logits,
        grad_gate,
        grad_up,
        grad_down,
    ) = run_experts(
        attended,
        w_output,
        x_block,
        gain_moe[None],
        g_all,
        w_gate,
        w_up,
        w_down,
        jnp.pad(router, pad),
        mask,
        3,
    )
    w_head_output = w_head_output.reshape(width, LANES)
    tiny_all = tiny_all.reshape(ep_count, 8, rows)
    gate_grad_rows = tiny_all[:, :local_experts].reshape(expert_count, rows).T
    row_terms = jnp.sum(tiny_all[:, local_experts], axis=0)[:, None]

    def own_micro(values):
        return lax.dynamic_index_in_dim(values, micro, keepdims=False)

    logits_own = logits
    scale_own = logits_own[:, expert_count : expert_count + 1]
    logits_own = logits_own[:, :expert_count]
    mask_rows = own_micro(mask)[:, :expert_count].astype(f32)
    probs_own = jax.nn.softmax(logits_own, axis=-1)
    prob_grad = gate_grad_rows * mask_rows
    logit_grad = (
        probs_own * (prob_grad - jnp.sum(probs_own * prob_grad, axis=1, keepdims=True))
    ).astype(bf16)
    router_block = lax.dynamic_slice_in_dim(router, block * LANES, LANES, axis=0)
    logit_grad_float = logit_grad.astype(f32)
    row_terms = row_terms + jnp.sum(logit_grad_float * logits_own, axis=1, keepdims=True)
    grad_router_part = contract_rows(
        (logit_grad_float * scale_own).astype(bf16), middle_gained
    )
    normed_grad_block = normed_grad_block + scale_own * contract_cols(logit_grad, router_block)
    grad_block = lax.dynamic_index_in_dim(column_block(g_all, block), micro, axis=1, keepdims=False)
    grad_block = grad_block.transpose(1, 0, 2, 3).reshape(rows, LANES).astype(f32)
    middle_grad = (
        grad_block
        + gain_moe * normed_grad_block
        - middle * (scale_own * scale_own * row_terms / width)
    )
    grad_gain_moe = jnp.sum(normed_grad_block * middle, axis=0)
    pack = jnp.concatenate(
        [
            grad_router_part,
            jnp.zeros((1, LANES), f32),
            grad_gain_moe[None],
            jnp.zeros((24 - 2 - expert_count, LANES), f32),
        ],
        axis=0,
    )

    grad_pieces, out_rows, input_grad_rows, packs = run_backward(
        middle_grad.astype(bf16),
        out_part,
        normed_in,
        w_heads,
        w_head_output,
        [
            middle_grad,
            queries,
            keys,
            value_rows,
            attended,
            query_pre,
            key_pre,
            x_block,
            jnp.stack(
                [
                    scales[0],
                    scales[1],
                    as_tiles(scale_in[:, 0]),
                    as_tiles(valid_rows.reshape(rows)),
                ]
            ),
            tables,
            valid_rows,
            gains_block,
            pack,
        ],
        5,
    )
    packs = jnp.sum(packs, axis=0)
    own_block = column_block(packs, ep_index, width // ep_count)
    head_rows = packs[expert_count + 2 : expert_count + 4].reshape(2, 2, 2, 2, 2, LANES)
    head_rows = head_rows.transpose(0, 4, 1, 2, 3, 5).reshape(2, width)
    own_head = column_block(head_rows, ep_index, width // ep_count)
    weight_grads = [
        grad_pieces[0, m].astype(f32) + grad_pieces[1, m].astype(f32) for m in range(4)
    ]
    return (
        out_rows.transpose(0, 2, 1, 3),
        input_grad_rows.transpose(0, 2, 1, 3).astype(f32),
        *weight_grads,
        own_block[:expert_count].T,
        own_block[expert_count],
        own_block[expert_count + 1],
        own_head[0],
        own_head[1],
        grad_gate,
        grad_up,
        grad_down,
    )


def shards(inputs, lengths, routes, *rest):
    sizes = (lax.axis_size("ep"), lax.axis_size("tp"), inputs.shape[0])
    local_heads = rest[0].shape[1] // HEAD_DIM
    if sizes == (8, 4, 2) and local_heads == 4:
        return cube_shards(inputs, lengths, routes, *rest)
    return routed_shards(inputs, lengths, routes, *rest)


def solution(mesh):
    return jax.shard_map(
        shards,
        mesh=mesh,
        in_specs=(
            P(None, "ep", None, None),
            P(),
            P(None, "ep", None, None),
            P("ep", "tp"),
            P("ep", "tp"),
            P("ep", "tp"),
            P("ep", "tp"),
            P("ep", None),
            P("ep"),
            P("ep"),
            P("ep"),
            P("ep"),
            P("ep", None, "tp"),
            P("ep", None, "tp"),
            P("ep", "tp", None),
            P(None, "ep", None, None),
        ),
        out_specs=(
            P(None, "ep", None, None),
            P(None, "ep", None, None),
            P("ep", "tp"),
            P("ep", "tp"),
            P("ep", "tp"),
            P("ep", "tp"),
            P("ep", None),
            P("ep"),
            P("ep"),
            P("ep"),
            P("ep"),
            P("ep", None, "tp"),
            P("ep", None, "tp"),
            P("ep", "tp", None),
        ),
        check_vma=False,
    )
```
